32 devices in a mesh: grp: 2 (over y), ctx: 4 (over z), exp: 2 (over x), tp: 2 (over core).
Axes of the slice: x: 2, y: 2, z: 4, core: 2. Of those that a mesh axis runs over, the one named last changes fastest.
Arguments:
- queries: bfloat16 [512, 6144], P(('grp', 'ctx'), ('exp', 'tp')), parts along dimension 0, may hold values from -16 to 16
- rotated_key_heads: bfloat16 [512, 1024], P(('grp', 'ctx'), ('exp', 'tp')), parts along dimension 0, may hold values from -16 to 16
- stored_value_heads: bfloat16 [512, 1024], P(('grp', 'ctx'), ('exp', 'tp')), parts along dimension 0, may hold values from -6 to 6
- block_order: int32 [16], P('grp'), parts along dimension 0, may hold values from 0 to 7, each once
- residual: bfloat16 [512, 6144], P(('grp', 'ctx', 'exp', 'tp')), parts along dimension 0, may hold values from -10 to 10
- out_weight: bfloat16 [6144, 6144], P(('exp', 'tp'), 'ctx'), may hold values from -0.5 to 0.5
- norm_gain: bfloat16 [6144], replicated, may hold values from 0.099609375 to 1.8984375
- expert_ids: int32 [512, 2], P(('grp', 'ctx', 'exp', 'tp')), parts along dimension 0, may hold values from 0 to 3, all different within a row; in each aligned block of 16 rows (0 to 15, 16 to 31, ...) at most 12 rows name the same one
- gate_logits: float32 [512, 2], P(('grp', 'ctx', 'exp', 'tp')), parts along dimension 0, may hold values from -6 to 6
- w_gate: bfloat16 [4, 6144, 8192], P('exp', None, ('ctx', 'tp')), may hold values from -0.078125 to 0.078125
- w_up: bfloat16 [4, 6144, 8192], P('exp', None, ('ctx', 'tp')), may hold values from -0.078125 to 0.078125
- w_down: bfloat16 [4, 8192, 6144], P('exp', ('ctx', 'tp')), may hold values from -0.0625 to 0.0625
Outputs:
- layer_out: bfloat16 [512, 6144], P(('grp', 'ctx', 'exp', 'tp')), parts along dimension 0
The draws below stay inside these ranges and needn't reach their ends.
There are 2 independent parts, one for each index of `grp`. The reference program is written for one: setup_inputs(seed, part) draws one part's arguments, and reference() takes and returns one part's arrays. A program takes and returns all parts, laid end to end along the dimension named above; an argument that names none is the same for every part. Nothing has to cross between parts.
Inputs may be any that keep to these rules, and one draw needn't show every extreme that they name: `expert_ids`: in the rows of one device (aligned blocks of 16 rows) each expert is named by at most 12 rows, a bound that some block reaches; the two ids of a row differ. A permutation: stored block b holds the positions block_order[b] * 32 onward, in order.
All inputs are finite; a program needn't handle non-finite values.
Results may differ from the reference program's by a relative error of at most 0.014.
Values may be sent and summed in bfloat16 or wider, within the bound.
A program may use at most 256 MiB of HBM per device.

```python
import math
import jax
import jax.numpy as jnp
import numpy as np
from jax import lax

D = 6144
QUERY_HEADS = 48
KEY_VALUE_HEADS = 8
HEAD_SIZE = 128
FF = 8192
EXPERTS = 4
TOP = 2
BLOCK = 32
SEQUENCE_TOKENS = 256
TOK_DEV = 16
CAP = 12
N_CTX = 4
N_TP = 2


def draw_queries(key, part):
    key = jax.random.fold_in(key, 22)
    return jax.random.truncated_normal(key, -4.0, 4.0, (SEQUENCE_TOKENS, QUERY_HEADS * HEAD_SIZE), jnp.float32).astype(jnp.bfloat16)


def draw_rotated_key_heads(key, part):
    key = jax.random.fold_in(key, 21)
    return jax.random.truncated_normal(key, -4.0, 4.0, (SEQUENCE_TOKENS, KEY_VALUE_HEADS * HEAD_SIZE), jnp.float32).astype(jnp.bfloat16)


def draw_residual(key, part):
    key = jax.random.fold_in(key, 7)
    return jax.random.truncated_normal(key, -6.0, 6.0, (SEQUENCE_TOKENS, D), jnp.float32).astype(jnp.bfloat16)


def levels(own_key, extent, shards, least, top_value):
    def one(position, blocks):
        heights = jax.random.uniform(jax.random.fold_in(jax.random.fold_in(own_key, 6), position), (blocks,), jnp.float32, least / len(shards), top_value / len(shards))
        return jnp.repeat(jnp.exp(heights), extent[position] // blocks).reshape((-1,) + (1,) * (len(extent) - position - 1))

    loudness = one(*shards[0])
    for cut in shards[1:]:
        loudness = loudness * one(*cut)
    return loudness


def shared_out(stream_key, own, number, rows, amount, top, limit, skew):
    order = jax.random.permutation(stream_key, amount)
    packed, usual = portions_of(amount, rows * top, limit, skew, True), portions_of(amount, rows * top, limit, skew, False)
    places = jnp.arange(amount)

    def named(sizes, offset_by):
        used = int((sizes > 0).sum())
        fixed = max(1, used // 4)
        passed = fixed + (places - fixed + offset_by * (used - fixed)) % max(1, amount - fixed)
        return jnp.zeros((amount,), jnp.int32).at[order[jnp.where(places < fixed, places, passed)]].set(jnp.asarray(sizes, jnp.int32))

    sizes = jnp.where(number % 4 == 0, named(packed, number // 4), named(usual, number - number // 4 - 1))
    mixed = jax.random.permutation(jax.random.fold_in(own, 3), amount)
    donor, taker = mixed[0:amount // 2 * 2:2], mixed[1:amount // 2 * 2:2]
    slack = jnp.minimum(sizes[donor] - 1, limit - sizes[taker]) // 2
    slack = jnp.where((donor == order[0]) | (taker == order[0]) | (sizes[taker] == 0), 0, jnp.maximum(slack, 0))
    passed = jax.random.randint(jax.random.fold_in(own, 4), (amount // 2,), 0, 1 << 20) % (slack + 1)
    sizes = sizes.at[donor].add(-passed).at[taker].add(passed)
    items = jnp.searchsorted(jnp.cumsum(sizes), jnp.arange(rows * top), side="right").astype(jnp.int32)
    grid = items.reshape(top, rows).T
    grid = grid[jax.random.permutation(jax.random.fold_in(own, 1), rows)]
    offset_by = jax.random.randint(jax.random.fold_in(own, 2), (rows, 1), 0, top)
    return jnp.take_along_axis(grid, (jnp.arange(top)[None, :] + offset_by) % top, axis=1)


def portions_of(count, total, bound, slope, full):
    weights = [(1 << 20) // math.isqrt(grade ** slope) + 1 for grade in range(1, count + 1)]
    largest = bound if full else min(bound, max(-(-total // count), total * weights[0] // sum(weights)))
    least = 1 if total - largest >= count - 1 else 0
    given, rest = [largest] + [least] * (count - 1), total - largest - least * (count - 1)
    while rest > 0:
        candidates = [i for i in range(1, count) if given[i] < largest] or [i for i in range(1, count) if given[i] < bound]
        mass, budget = sum([weights[i] for i in candidates]), rest
        for i in candidates:
            more = min(bound - given[i], max(1, budget * weights[i] // mass), rest)
            given[i] = given[i] + more
            rest = rest - more
    return np.array(given)


def bell_draw(rng, shape, deviation, most, cuts=(), kind=jnp.bfloat16):
    values = jax.random.normal(rng, shape, jnp.float32) * deviation
    if len(cuts) > 0:
        values = levels(rng, shape, cuts, -0.22, 0.18) * values
    return jnp.clip(values, min=-most, max=most).astype(kind)


def setup_inputs(seed: int = 0, part: int = 0) -> dict:
    streams_of = jax.random.split(jax.random.key(seed), 13)
    part_splits = jax.random.split(jax.random.fold_in(streams_of[12], part), 13)
    queries = draw_queries(jax.random.fold_in(jax.random.fold_in(streams_of[12], part), 71), part)
    rotated_key_heads = draw_rotated_key_heads(jax.random.fold_in(jax.random.fold_in(streams_of[12], part), 71), part)
    stored_value_heads = bell_draw(part_splits[2], (SEQUENCE_TOKENS, KEY_VALUE_HEADS * HEAD_SIZE), 1.0, 6.0, ((0, 4), (1, 4)))
    block_order = jax.random.permutation(part_splits[3], 2 * N_CTX).astype(jnp.int32)
    residual = draw_residual(jax.random.fold_in(jax.random.fold_in(streams_of[12], part), 71), part)
    out_weight = bell_draw(streams_of[5], (QUERY_HEADS * HEAD_SIZE, D), HEAD_SIZE ** -0.5, 0.5, ((0, 4), (1, 4)))
    norm_gain = jnp.clip(1.0 + 0.18 * jax.random.normal(streams_of[6], (D,), jnp.float32), 0.099609375, 1.8984375).astype(jnp.bfloat16)
    expert_ids_keys = jax.random.split(jax.random.fold_in(part_splits[7], 1), SEQUENCE_TOKENS // TOK_DEV)
    expert_ids_turns = jax.random.permutation(jax.random.fold_in(part_splits[7], 3), SEQUENCE_TOKENS // TOK_DEV)
    expert_ids = jax.vmap(lambda own, number: shared_out(jax.random.fold_in(part_splits[7], 2), own, number, TOK_DEV, EXPERTS, TOP, CAP, 2))(expert_ids_keys, expert_ids_turns).reshape((SEQUENCE_TOKENS, TOP))
    gate_logits = bell_draw(part_splits[8], (SEQUENCE_TOKENS, TOP), 1.5, 6.0, ((0, 16),), jnp.float32)
    w_gate = bell_draw(streams_of[9], (EXPERTS, D, FF), D ** -0.5, 0.078125, ((0, 2), (2, 8)))
    w_up = bell_draw(streams_of[10], (EXPERTS, D, FF), D ** -0.5, 0.078125, ((0, 2), (2, 8)))
    w_down = bell_draw(streams_of[11], (EXPERTS, FF, D), FF ** -0.5, 0.0625, ((0, 2), (1, 8)))
    return dict(queries=queries, rotated_key_heads=rotated_key_heads, stored_value_heads=stored_value_heads, block_order=block_order, residual=residual, out_weight=out_weight, norm_gain=norm_gain, expert_ids=expert_ids, gate_logits=gate_logits, w_gate=w_gate, w_up=w_up, w_down=w_down)


def reference(queries, rotated_key_heads, stored_value_heads, block_order, residual, out_weight, norm_gain, expert_ids, gate_logits, w_gate, w_up, w_down):
    row_index = jnp.arange(SEQUENCE_TOKENS, dtype=jnp.int32)
    token_pos = block_order[row_index // BLOCK] * BLOCK + row_index % BLOCK
    allowed = token_pos[None, :] <= token_pos[:, None]
    query_group_width = QUERY_HEADS // KEY_VALUE_HEADS
    score_scale = 1.0 / math.sqrt(HEAD_SIZE)
    query_head_table = jnp.transpose(queries.reshape(SEQUENCE_TOKENS, KEY_VALUE_HEADS, query_group_width, HEAD_SIZE), (1, 0, 2, 3))
    key_head_table = jnp.transpose(rotated_key_heads.reshape(SEQUENCE_TOKENS, KEY_VALUE_HEADS, HEAD_SIZE), (1, 0, 2))
    value_head_table = jnp.transpose(stored_value_heads.reshape(SEQUENCE_TOKENS, KEY_VALUE_HEADS, HEAD_SIZE), (1, 0, 2))

    def one_head(inputs):
        query_block, key_block, value_block = inputs
        scores = jnp.einsum('tgd,sd->gts', query_block.astype(jnp.float32), key_block.astype(jnp.float32), precision=lax.Precision.HIGHEST) * score_scale
        scores = jnp.where(allowed[None], scores, -1e+30)
        top_score = lax.optimization_barrier(jnp.max(scores, axis=-1, keepdims=True))
        weights = jnp.where(allowed[None], jnp.exp(scores - top_score), 0.0)
        weight_total = lax.optimization_barrier(jnp.sum(weights, axis=-1))
        mixed_heads = jnp.einsum('gts,sd->gtd', weights, value_block.astype(jnp.float32), precision=lax.Precision.HIGHEST)
        return mixed_heads / weight_total[..., None]
    per_head = lax.map(one_head, (query_head_table, key_head_table, value_head_table))
    attended = jnp.transpose(per_head, (2, 0, 1, 3)).reshape(SEQUENCE_TOKENS, QUERY_HEADS * HEAD_SIZE).astype(jnp.bfloat16)
    projected = jnp.dot(attended, out_weight, preferred_element_type=jnp.float32)
    hidden_state = (residual.astype(jnp.float32) + projected).astype(jnp.bfloat16)
    state_f32 = hidden_state.astype(jnp.float32)
    normed = (state_f32 * lax.rsqrt(lax.optimization_barrier(jnp.mean(state_f32 * state_f32, axis=-1, keepdims=True)) + 1e-05) * norm_gain.astype(jnp.float32)).astype(jnp.bfloat16)
    shard_count = N_CTX * N_TP
    shard_width = FF // shard_count
    first_weight = jax.nn.sigmoid(gate_logits[:, 0] - gate_logits[:, 1])
    second_weight = jax.nn.sigmoid(gate_logits[:, 1] - gate_logits[:, 0])
    mixture = jnp.zeros((SEQUENCE_TOKENS, D), jnp.float32)
    for expert in range(EXPERTS):
        gate_val = jnp.dot(normed, w_gate[expert], preferred_element_type=jnp.float32)
        up_val = jnp.dot(normed, w_up[expert], preferred_element_type=jnp.float32)
        active = (jax.nn.silu(gate_val) * up_val).astype(jnp.bfloat16)
        down_rows = w_down[expert]

        def add_shard(running, shard_index):
            begin_at = (shard_index * shard_width).astype(jnp.int32)
            shard_term = jnp.dot(lax.dynamic_slice_in_dim(active, begin_at, shard_width, 1), lax.dynamic_slice_in_dim(down_rows, begin_at, shard_width, 0), preferred_element_type=jnp.float32)
            rounded = lax.optimization_barrier(shard_term.astype(jnp.bfloat16))
            return (running + rounded.astype(jnp.float32), None)
        summed, unused = lax.scan(add_shard, jnp.zeros((SEQUENCE_TOKENS, D), jnp.float32), jnp.arange(shard_count, dtype=jnp.int32))
        expert_out = lax.optimization_barrier(summed.astype(jnp.bfloat16)).astype(jnp.float32)
        weight_row = first_weight * (expert_ids[:, 0] == expert).astype(jnp.float32) + second_weight * (expert_ids[:, 1] == expert).astype(jnp.float32)
        mixture = mixture + weight_row[:, None] * expert_out
    return (hidden_state.astype(jnp.float32) + mixture).astype(jnp.bfloat16)
```

```python
import math

import jax
import jax.numpy as jnp
from jax import lax
from jax.sharding import PartitionSpec as P

HEAD_SIZE = 128
EXPERTS = 4
BLOCK = 32
NEG_LARGE = -1e30


def positions(block_order, rows):
    return (block_order[:, None] * BLOCK + jnp.arange(BLOCK, dtype=jnp.int32)[None, :]).reshape(rows)


def attend(queries, keys, values, block_order):
    rows = queries.shape[0]
    kv_local = keys.shape[1] // HEAD_SIZE
    group = queries.shape[1] // keys.shape[1]
    pos = positions(block_order, rows)
    allowed = pos[None, :] <= pos[:, None]
    scale = 1.0 / math.sqrt(HEAD_SIZE)
    heads = []
    for k in range(kv_local):
        key = keys[:, k * HEAD_SIZE : (k + 1) * HEAD_SIZE]
        value = values[:, k * HEAD_SIZE : (k + 1) * HEAD_SIZE]
        q = queries[:, k * group * HEAD_SIZE : (k + 1) * group * HEAD_SIZE].reshape(rows, group, HEAD_SIZE)
        scores = jnp.einsum("tgd,sd->gts", q, key, preferred_element_type=jnp.float32) * scale
        scores = jnp.where(allowed[None], scores, NEG_LARGE)
        weights = jnp.exp(scores - jnp.max(scores, axis=-1, keepdims=True))
        total = jnp.sum(weights, axis=-1, keepdims=True)
        mixed = jnp.einsum(
            "gts,sd->gtd", weights.astype(jnp.bfloat16), value, preferred_element_type=jnp.float32
        )
        heads.append(jnp.transpose((mixed / total).astype(jnp.bfloat16), (1, 0, 2)).reshape(rows, -1))
    return jnp.concatenate(heads, axis=1)


def shards(
    queries,
    rotated_key_heads,
    stored_value_heads,
    block_order,
    residual,
    out_weight,
    norm_gain,
    expert_ids,
    gate_logits,
    w_gate,
    w_up,
    w_down,
):
    ctx, exp, tp = (lax.axis_size(name) for name in ("ctx", "exp", "tp"))
    tok_rows, width = residual.shape
    local_experts = EXPERTS // exp
    all_axes = ("ctx", "exp", "tp")

    first = jax.nn.sigmoid(gate_logits[:, 0] - gate_logits[:, 1])
    second = jax.nn.sigmoid(gate_logits[:, 1] - gate_logits[:, 0])
    names = jnp.arange(EXPERTS, dtype=jnp.int32)[None, :]
    row_gates = first[:, None] * (expert_ids[:, :1] == names) + second[:, None] * (expert_ids[:, 1:] == names)
    gates = lax.all_gather(row_gates, all_axes, axis=0, tiled=True)

    qw, kw = queries.shape[1], rotated_key_heads.shape[1]
    own = jnp.concatenate([queries, rotated_key_heads, stored_value_heads], axis=1)
    qkv = lax.all_gather(own, "ctx", axis=0, tiled=True)
    attended = attend(qkv[:, :qw], qkv[:, qw : qw + kw], qkv[:, qw + kw :], block_order)
    part = jnp.dot(attended, out_weight, preferred_element_type=jnp.float32).astype(jnp.bfloat16)
    part = part.reshape(ctx, exp * tp, tok_rows, -1)
    part = lax.psum_scatter(part, ("exp", "tp"), scatter_dimension=1, tiled=True)
    part = part.reshape(ctx, tok_rows, -1)
    part = lax.all_to_all(part, "ctx", split_axis=0, concat_axis=0, tiled=True)
    projected = jnp.transpose(part, (1, 0, 2)).reshape(tok_rows, width).astype(jnp.float32)
    hidden_state = (residual.astype(jnp.float32) + projected).astype(jnp.bfloat16)
    state = hidden_state.astype(jnp.float32)
    normed = (
        state
        * lax.rsqrt(jnp.mean(state * state, axis=-1, keepdims=True) + 1e-05)
        * norm_gain.astype(jnp.float32)
    ).astype(jnp.bfloat16)

    rows = lax.all_gather(normed, all_axes, axis=0, tiled=True)
    base = lax.axis_index("exp") * local_experts
    actives = []
    gate_val = jnp.einsum("rd,edf->erf", rows, w_gate, preferred_element_type=jnp.float32)
    up_val = jnp.einsum("rd,edf->erf", rows, w_up, preferred_element_type=jnp.float32)
    local_gates = lax.dynamic_slice_in_dim(gates, base, local_experts, axis=1)
    active = (jax.nn.silu(gate_val) * up_val * local_gates.T[:, :, None]).astype(jnp.bfloat16)
    active = jnp.transpose(active, (1, 0, 2)).reshape(rows.shape[0], -1)
    sums = jnp.dot(active, w_down.reshape(-1, width), preferred_element_type=jnp.float32)
    mixture = lax.psum_scatter(sums.astype(jnp.bfloat16), all_axes, scatter_dimension=0, tiled=True)
    return (state + mixture.astype(jnp.float32)).astype(jnp.bfloat16)


def solution(mesh):
    placed = (
        P(("grp", "ctx"), ("exp", "tp")),
        P(("grp", "ctx"), ("exp", "tp")),
        P(("grp", "ctx"), ("exp", "tp")),
        P("grp"),
        P(("grp", "ctx", "exp", "tp"), None),
        P(("exp", "tp"), "ctx"),
        P(),
        P(("grp", "ctx", "exp", "tp"), None),
        P(("grp", "ctx", "exp", "tp"), None),
        P("exp", None, ("ctx", "tp")),
        P("exp", None, ("ctx", "tp")),
        P("exp", ("ctx", "tp"), None),
    )
    return jax.shard_map(
        shards,
        mesh=mesh,
        in_specs=placed,
        out_specs=P(("grp", "ctx", "exp", "tp"), None),
        check_vma=False,
    )
```

```python
import functools
import math

import jax
import jax.numpy as jnp
from jax import lax
from jax.experimental import pallas as pl
from jax.experimental.pallas import tpu as pltpu
from jax.sharding import PartitionSpec as P

HEAD_SIZE = 128
EXPERTS = 4
BLOCK = 32
NEG_LARGE = -1e30


def positions(block_order, rows):
    return (block_order[:, None] * BLOCK + jnp.arange(BLOCK, dtype=jnp.int32)[None, :]).reshape(rows)


def attend(queries, keys, values, block_order):
    rows = queries.shape[0]
    kv_local = keys.shape[1] // HEAD_SIZE
    group = queries.shape[1] // keys.shape[1]
    pos = positions(block_order, rows)
    allowed = pos[None, :] <= pos[:, None]
    scale = 1.0 / math.sqrt(HEAD_SIZE)
    heads = []
    for k in range(kv_local):
        key = keys[:, k * HEAD_SIZE : (k + 1) * HEAD_SIZE]
        value = values[:, k * HEAD_SIZE : (k + 1) * HEAD_SIZE]
        q = queries[:, k * group * HEAD_SIZE : (k + 1) * group * HEAD_SIZE].reshape(rows, group, HEAD_SIZE)
        scores = jnp.einsum("tgd,sd->gts", q, key, preferred_element_type=jnp.float32) * scale
        scores = jnp.where(allowed[None], scores, NEG_LARGE)
        weights = jnp.exp(scores - jnp.max(scores, axis=-1, keepdims=True))
        total = jnp.sum(weights, axis=-1, keepdims=True)
        mixed = jnp.einsum(
            "gts,sd->gtd", weights.astype(jnp.bfloat16), value, preferred_element_type=jnp.float32
        )
        heads.append(jnp.transpose((mixed / total).astype(jnp.bfloat16), (1, 0, 2)).reshape(rows, -1))
    return jnp.concatenate(heads, axis=1)


MESH = pl.DeviceIdType.MESH
LANES = 128
VMEM_LIMIT = 48 * 1024 * 1024


def remote(src, dst, send_sem, recv_sem, device):
    return pltpu.make_async_remote_copy(
        src_ref=src, dst_ref=dst, send_sem=send_sem, recv_sem=recv_sem, device_id=device, device_id_type=MESH
    )


def greet(devices):
    barrier = pltpu.get_barrier_semaphore()
    for device in devices:
        pl.semaphore_signal(barrier, inc=1, device_id=device, device_id_type=MESH)
    pl.semaphore_wait(barrier, len(devices))


def swap_kernel(ctx, exp, tp, part, gates, projected, all_gates, got, got_gates, sends, recvs, gate_sends, gate_recvs):
    count = ctx * exp * tp
    me = (lax.axis_index("ctx") * exp + lax.axis_index("exp")) * tp + lax.axis_index("tp")
    peers, devices = [], []
    for offset in range(1, count):
        peer = lax.rem(me + offset, count)
        peers.append(peer)
        devices.append(
            {"ctx": lax.div(peer, exp * tp), "exp": lax.rem(lax.div(peer, tp), exp), "tp": lax.rem(peer, tp)}
        )
    greet(devices)
    copies = []
    for i, (peer, device) in enumerate(zip(peers, devices)):
        copies.append(remote(part.at[peer], got.at[me], sends.at[i], recvs.at[i], device))
        copies[-1].start()
    gate_copies = []
    for i, device in enumerate(devices):
        gate_copies.append(remote(gates, got_gates.at[me], gate_sends.at[i], gate_recvs.at[i], device))
        gate_copies[-1].start()
    got[me] = part[me]
    got_gates[me] = gates[...]
    for copy in copies + gate_copies:
        copy.wait()
    columns = part.shape[2]
    for c in range(ctx):
        total = got[c * exp * tp].astype(jnp.float32)
        for j in range(1, exp * tp):
            total += got[c * exp * tp + j].astype(jnp.float32)
        projected[:, c * columns : (c + 1) * columns] = total
    all_gates[...] = got_gates[...]


def swap(part, gates, ctx, exp, tp):
    count, tok_rows, columns = part.shape
    whole = pl.BlockSpec(memory_space=pltpu.VMEM)
    return pl.pallas_call(
        functools.partial(swap_kernel, ctx, exp, tp),
        out_shape=[
            jax.ShapeDtypeStruct((tok_rows, ctx * columns), jnp.float32),
            jax.ShapeDtypeStruct((count, tok_rows, LANES), jnp.float32),
        ],
        in_specs=[whole] * 2,
        out_specs=[whole] * 2,
        scratch_shapes=[
            pltpu.VMEM((count, tok_rows, columns), jnp.bfloat16),
            pltpu.VMEM((count, tok_rows, LANES), jnp.float32),
        ]
        + [pltpu.SemaphoreType.DMA((count - 1,))] * 4,
        compiler_params=pltpu.CompilerParams(
            collective_id=0, has_side_effects=True, vmem_limit_bytes=VMEM_LIMIT
        ),
    )(part, gates)


def reduce_kernel(ctx, exp, tp, sums, out, got1, acc1, got2, acc2, got3, s1, v1, s2, v2, s3, v3):
    c, e, t = lax.axis_index("ctx"), lax.axis_index("exp"), lax.axis_index("tp")
    pair = lax.rem(t + 1, tp)
    cs = [lax.rem(c + k, ctx) for k in range(ctx)]
    es = [lax.rem(e + k, exp) for k in range(exp)]

    def device(cc, ee, tt):
        return {"ctx": cc, "exp": ee, "tp": tt}

    greet(
        [device(c, e, pair)]
        + [device(c, es[j], t) for j in range(1, exp)]
        + [device(cs[k], e, t) for k in range(1, ctx)]
    )
    order = list(range(1, ctx)) + [0]
    first, second, third = {}, {}, {}
    for j in list(range(1, exp)) + [0]:
        for k in order:
            first[k, j] = remote(
                sums.at[cs[k], es[j], pair], got1.at[k, j], s1.at[k, j], v1.at[k, j], device(c, e, pair)
            )
            first[k, j].start()
    for k in order:
        for j in range(1, exp):
            first[k, j].wait_recv()
            acc1[j - 1, k] = (
                sums[cs[k], es[j], t].astype(jnp.float32) + got1[k, j].astype(jnp.float32)
            ).astype(jnp.bfloat16)
            second[k, j] = remote(
                acc1.at[j - 1, k], got2.at[j - 1, k], s2.at[j - 1, k], v2.at[j - 1, k], device(c, es[j], t)
            )
            second[k, j].start()
    for k in order:
        first[k, 0].wait_recv()
        total = sums[cs[k], e, t].astype(jnp.float32) + got1[k, 0].astype(jnp.float32)
        for j in range(1, exp):
            second[k, j].wait_recv()
            total += got2[j - 1, k].astype(jnp.float32)
        if k > 0:
            acc2[k - 1] = total.astype(jnp.bfloat16)
            third[k] = remote(
                acc2.at[k - 1], got3.at[k - 1], s3.at[k - 1], v3.at[k - 1], device(cs[k], e, t)
            )
            third[k].start()
        else:
            out[...] = total
    for k in range(1, ctx):
        third[k].wait_recv()
        out[...] += got3[k - 1].astype(jnp.float32)
    for copy in list(first.values()) + list(second.values()) + list(third.values()):
        copy.wait_send()


def reduce_rows(sums):
    ctx, exp, tp, tok_rows, width = sums.shape
    whole = pl.BlockSpec(memory_space=pltpu.VMEM)
    block = (tok_rows, width)
    return pl.pallas_call(
        functools.partial(reduce_kernel, ctx, exp, tp),
        out_shape=jax.ShapeDtypeStruct(block, jnp.float32),
        in_specs=[whole],
        out_specs=whole,
        scratch_shapes=[
            pltpu.VMEM((ctx, exp) + block, jnp.bfloat16),
            pltpu.VMEM((exp - 1, ctx) + block, jnp.bfloat16),
            pltpu.VMEM((exp - 1, ctx) + block, jnp.bfloat16),
            pltpu.VMEM((ctx - 1,) + block, jnp.bfloat16),
            pltpu.VMEM((ctx - 1,) + block, jnp.bfloat16),
            pltpu.SemaphoreType.DMA((ctx, exp)),
            pltpu.SemaphoreType.DMA((ctx, exp)),
            pltpu.SemaphoreType.DMA((exp - 1, ctx)),
            pltpu.SemaphoreType.DMA((exp - 1, ctx)),
            pltpu.SemaphoreType.DMA((ctx - 1,)),
            pltpu.SemaphoreType.DMA((ctx - 1,)),
        ],
        compiler_params=pltpu.CompilerParams(
            collective_id=1, has_side_effects=True, vmem_limit_bytes=VMEM_LIMIT
        ),
    )(sums)


def down_kernel(active, weights, out):
    out[...] = jnp.dot(active[...], weights[...], preferred_element_type=jnp.float32).astype(jnp.bfloat16)


def down(active, weights):
    rows, hidden = active.shape
    width = weights.shape[1]
    tile = 512
    return pl.pallas_call(
        down_kernel,
        grid=(width // tile,),
        out_shape=jax.ShapeDtypeStruct((rows, width), jnp.bfloat16),
        in_specs=[
            pl.BlockSpec((rows, hidden), lambda i: (0, 0)),
            pl.BlockSpec((hidden, tile), lambda i: (0, i)),
        ],
        out_specs=pl.BlockSpec((rows, tile), lambda i: (0, i)),
        compiler_params=pltpu.CompilerParams(vmem_limit_bytes=VMEM_LIMIT),
    )(active, weights)


def shards(
    queries,
    rotated_key_heads,
    stored_value_heads,
    block_order,
    residual,
    out_weight,
    norm_gain,
    expert_ids,
    gate_logits,
    w_gate,
    w_up,
    w_down,
):
    ctx, exp, tp = (lax.axis_size(name) for name in ("ctx", "exp", "tp"))
    tok_rows, width = residual.shape
    local_experts = EXPERTS // exp
    all_axes = ("ctx", "exp", "tp")

    first = jax.nn.sigmoid(gate_logits[:, 0] - gate_logits[:, 1])
    second = jax.nn.sigmoid(gate_logits[:, 1] - gate_logits[:, 0])
    names = jnp.arange(EXPERTS, dtype=jnp.int32)[None, :]
    row_gates = first[:, None] * (expert_ids[:, :1] == names) + second[:, None] * (expert_ids[:, 1:] == names)

    qw, kw = queries.shape[1], rotated_key_heads.shape[1]
    own = jnp.concatenate([queries, rotated_key_heads, stored_value_heads], axis=1)
    qkv = lax.all_gather(own, "ctx", axis=0, tiled=True)
    attended = attend(qkv[:, :qw], qkv[:, qw : qw + kw], qkv[:, qw + kw :], block_order)
    part = jnp.dot(attended, out_weight, preferred_element_type=jnp.float32).astype(jnp.bfloat16)
    projected, gates = swap(
        part.reshape(ctx * exp * tp, tok_rows, -1),
        jnp.pad(row_gates, ((0, 0), (0, LANES - EXPERTS))),
        ctx,
        exp,
        tp,
    )
    gates = gates.reshape(-1, LANES)
    hidden_state = (residual.astype(jnp.float32) + projected).astype(jnp.bfloat16)
    state = hidden_state.astype(jnp.float32)
    normed = (
        state
        * lax.rsqrt(jnp.mean(state * state, axis=-1, keepdims=True) + 1e-05)
        * norm_gain.astype(jnp.float32)
    ).astype(jnp.bfloat16)

    rows = lax.all_gather(normed, all_axes, axis=0, tiled=True)
    base = lax.axis_index("exp") * local_experts
    gate_val = jnp.einsum("rd,edf->erf", rows, w_gate, preferred_element_type=jnp.float32)
    up_val = jnp.einsum("rd,edf->erf", rows, w_up, preferred_element_type=jnp.float32)
    local_gates = lax.dynamic_slice_in_dim(gates, base, local_experts, axis=1)
    active = (jax.nn.silu(gate_val) * up_val * local_gates.T[:, :, None]).astype(jnp.bfloat16)
    active = jnp.transpose(active, (1, 0, 2)).reshape(rows.shape[0], -1)
    sums = down(active, w_down.reshape(-1, width))
    mixture = reduce_rows(sums.reshape(ctx, exp, tp, tok_rows, width))
    return (state + mixture).astype(jnp.bfloat16)


def solution(mesh):
    placed = (
        P(("grp", "ctx"), ("exp", "tp")),
        P(("grp", "ctx"), ("exp", "tp")),
        P(("grp", "ctx"), ("exp", "tp")),
        P("grp"),
        P(("grp", "ctx", "exp", "tp"), None),
        P(("exp", "tp"), "ctx"),
        P(),
        P(("grp", "ctx", "exp", "tp"), None),
        P(("grp", "ctx", "exp", "tp"), None),
        P("exp", None, ("ctx", "tp")),
        P("exp", None, ("ctx", "tp")),
        P("exp", ("ctx", "tp"), None),
    )
    return jax.shard_map(
        shards,
        mesh=mesh,
        in_specs=placed,
        out_specs=P(("grp", "ctx", "exp", "tp"), None),
        check_vma=False,
    )
```

```python
import functools
import math

import jax
import jax.numpy as jnp
from jax import lax
from jax.experimental import pallas as pl
from jax.experimental.pallas import tpu as pltpu
from jax.sharding import PartitionSpec as P

HEAD_SIZE = 128
EXPERTS = 4
BLOCK = 32
NEG_LARGE = -1e30


def positions(block_order, rows):
    return (block_order[:, None] * BLOCK + jnp.arange(BLOCK, dtype=jnp.int32)[None, :]).reshape(rows)


def attend(queries, keys, values, block_order):
    rows = queries.shape[0]
    kv_local = keys.shape[1] // HEAD_SIZE
    group = queries.shape[1] // keys.shape[1]
    pos = positions(block_order, rows)
    allowed = pos[None, :] <= pos[:, None]
    scale = 1.0 / math.sqrt(HEAD_SIZE)
    heads = []
    for k in range(kv_local):
        key = keys[:, k * HEAD_SIZE : (k + 1) * HEAD_SIZE]
        value = values[:, k * HEAD_SIZE : (k + 1) * HEAD_SIZE]
        q = queries[:, k * group * HEAD_SIZE : (k + 1) * group * HEAD_SIZE].reshape(rows, group, HEAD_SIZE)
        scores = jnp.einsum("tgd,sd->gts", q, key, preferred_element_type=jnp.float32) * scale
        scores = jnp.where(allowed[None], scores, NEG_LARGE)
        weights = jnp.exp(scores - jnp.max(scores, axis=-1, keepdims=True))
        total = jnp.sum(weights, axis=-1, keepdims=True)
        mixed = jnp.einsum(
            "gts,sd->gtd", weights.astype(jnp.bfloat16), value, preferred_element_type=jnp.float32
        )
        heads.append(jnp.transpose((mixed / total).astype(jnp.bfloat16), (1, 0, 2)).reshape(rows, -1))
    return jnp.concatenate(heads, axis=1)


MESH = pl.DeviceIdType.MESH
LANES = 128
VMEM_LIMIT = 48 * 1024 * 1024


def remote(src, dst, send_sem, recv_sem, device):
    return pltpu.make_async_remote_copy(
        src_ref=src, dst_ref=dst, send_sem=send_sem, recv_sem=recv_sem, device_id=device, device_id_type=MESH
    )


def greet(devices):
    barrier = pltpu.get_barrier_semaphore()
    for device in devices:
        pl.semaphore_signal(barrier, inc=1, device_id=device, device_id_type=MESH)
    pl.semaphore_wait(barrier, len(devices))


def swap_kernel(ctx, exp, tp, part, gates, projected, all_gates, got, got_gates, sends, recvs, gate_sends, gate_recvs):
    count = ctx * exp * tp
    me = (lax.axis_index("ctx") * exp + lax.axis_index("exp")) * tp + lax.axis_index("tp")
    peers, devices = [], []
    for offset in range(1, count):
        peer = lax.rem(me + offset, count)
        peers.append(peer)
        devices.append(
            {"ctx": lax.div(peer, exp * tp), "exp": lax.rem(lax.div(peer, tp), exp), "tp": lax.rem(peer, tp)}
        )
    greet(devices)
    copies = []
    for i, (peer, device) in enumerate(zip(peers, devices)):
        copies.append(remote(part.at[peer], got.at[me], sends.at[i], recvs.at[i], device))
        copies[-1].start()
    gate_copies = []
    for i, device in enumerate(devices):
        gate_copies.append(remote(gates, got_gates.at[me], gate_sends.at[i], gate_recvs.at[i], device))
        gate_copies[-1].start()
    got[me] = part[me]
    got_gates[me] = gates[...]
    for copy in copies + gate_copies:
        copy.wait()
    columns = part.shape[2]
    for c in range(ctx):
        total = got[c * exp * tp].astype(jnp.float32)
        for j in range(1, exp * tp):
            total += got[c * exp * tp + j].astype(jnp.float32)
        projected[:, c * columns : (c + 1) * columns] = total
    all_gates[...] = got_gates[...]


def swap(part, gates, ctx, exp, tp):
    count, tok_rows, columns = part.shape
    whole = pl.BlockSpec(memory_space=pltpu.VMEM)
    return pl.pallas_call(
        functools.partial(swap_kernel, ctx, exp, tp),
        out_shape=[
            jax.ShapeDtypeStruct((tok_rows, ctx * columns), jnp.float32),
            jax.ShapeDtypeStruct((count, tok_rows, LANES), jnp.float32),
        ],
        in_specs=[whole] * 2,
        out_specs=[whole] * 2,
        scratch_shapes=[
            pltpu.VMEM((count, tok_rows, columns), jnp.bfloat16),
            pltpu.VMEM((count, tok_rows, LANES), jnp.float32),
        ]
        + [pltpu.SemaphoreType.DMA((count - 1,))] * 4,
        compiler_params=pltpu.CompilerParams(
            collective_id=0, has_side_effects=True, vmem_limit_bytes=VMEM_LIMIT
        ),
    )(part, gates)


def reduce_kernel(ctx, exp, tp, sums, out, got1, acc1, got2, acc2, got3, s1, v1, s2, v2, s3, v3):
    c, e, t = lax.axis_index("ctx"), lax.axis_index("exp"), lax.axis_index("tp")
    pair = lax.rem(t + 1, tp)
    cs = [lax.rem(c + k, ctx) for k in range(ctx)]
    es = [lax.rem(e + k, exp) for k in range(exp)]

    def device(cc, ee, tt):
        return {"ctx": cc, "exp": ee, "tp": tt}

    greet(
        [device(c, e, pair)]
        + [device(c, es[j], t) for j in range(1, exp)]
        + [device(cs[k], e, t) for k in range(1, ctx)]
    )
    order = list(range(1, ctx)) + [0]
    first, second, third = {}, {}, {}
    for j in list(range(1, exp)) + [0]:
        for k in order:
            first[k, j] = remote(
                sums.at[cs[k], es[j], pair], got1.at[k, j], s1.at[k, j], v1.at[k, j], device(c, e, pair)
            )
            first[k, j].start()
    for k in order:
        for j in range(1, exp):
            first[k, j].wait_recv()
            acc1[j - 1, k] = (
                sums[cs[k], es[j], t].astype(jnp.float32) + got1[k, j].astype(jnp.float32)
            ).astype(jnp.bfloat16)
            second[k, j] = remote(
                acc1.at[j - 1, k], got2.at[j - 1, k], s2.at[j - 1, k], v2.at[j - 1, k], device(c, es[j], t)
            )
            second[k, j].start()
    for k in order:
        first[k, 0].wait_recv()
        total = sums[cs[k], e, t].astype(jnp.float32) + got1[k, 0].astype(jnp.float32)
        for j in range(1, exp):
            second[k, j].wait_recv()
            total += got2[j - 1, k].astype(jnp.float32)
        if k > 0:
            acc2[k - 1] = total.astype(jnp.bfloat16)
            third[k] = remote(
                acc2.at[k - 1], got3.at[k - 1], s3.at[k - 1], v3.at[k - 1], device(cs[k], e, t)
            )
            third[k].start()
        else:
            out[...] = total
    for k in range(1, ctx):
        third[k].wait_recv()
        out[...] += got3[k - 1].astype(jnp.float32)
    for copy in list(first.values()) + list(second.values()) + list(third.values()):
        copy.wait_send()


def reduce_rows(sums):
    ctx, exp, tp, tok_rows, width = sums.shape
    whole = pl.BlockSpec(memory_space=pltpu.VMEM)
    block = (tok_rows, width)
    return pl.pallas_call(
        functools.partial(reduce_kernel, ctx, exp, tp),
        out_shape=jax.ShapeDtypeStruct(block, jnp.float32),
        in_specs=[whole],
        out_specs=whole,
        scratch_shapes=[
            pltpu.VMEM((ctx, exp) + block, jnp.bfloat16),
            pltpu.VMEM((exp - 1, ctx) + block, jnp.bfloat16),
            pltpu.VMEM((exp - 1, ctx) + block, jnp.bfloat16),
            pltpu.VMEM((ctx - 1,) + block, jnp.bfloat16),
            pltpu.VMEM((ctx - 1,) + block, jnp.bfloat16),
            pltpu.SemaphoreType.DMA((ctx, exp)),
            pltpu.SemaphoreType.DMA((ctx, exp)),
            pltpu.SemaphoreType.DMA((exp - 1, ctx)),
            pltpu.SemaphoreType.DMA((exp - 1, ctx)),
            pltpu.SemaphoreType.DMA((ctx - 1,)),
            pltpu.SemaphoreType.DMA((ctx - 1,)),
        ],
        compiler_params=pltpu.CompilerParams(
            collective_id=1, has_side_effects=True, vmem_limit_bytes=VMEM_LIMIT
        ),
    )(sums)


def gather_kernel(ctx, exp, tp, own, out, s1, v1, s2, v2, s3, v3):
    c, e, t = lax.axis_index("ctx"), lax.axis_index("exp"), lax.axis_index("tp")
    pair = lax.rem(t + 1, tp)
    to_c = [lax.rem(c + k, ctx) for k in range(ctx)]
    from_c = [lax.rem(c + ctx - k, ctx) for k in range(ctx)]
    to_e = [lax.rem(e + j, exp) for j in range(exp)]
    from_e = [lax.rem(e + exp - j, exp) for j in range(exp)]
    near = {"ctx": c, "exp": e, "tp": pair}
    rows = [{"ctx": to_c[k], "exp": e, "tp": t} for k in range(1, ctx)]
    sides = [{"ctx": c, "exp": to_e[j], "tp": t} for j in range(1, exp)]
    greet([near] + rows + sides)
    out[c, e, t] = own[...]
    copies, first, second = [], {}, {}

    def send(cc, ee, send_sem, recv_sem, device):
        block = out.at[cc, ee, t]
        copy = remote(block, block, send_sem, recv_sem, device)
        copy.start()
        copies.append(copy)
        return copy

    for k in range(1, ctx):
        first[k] = send(c, e, s1.at[k - 1], v1.at[k - 1], rows[k - 1])
    third = []
    for k in range(ctx):
        if k > 0:
            first[k].wait_recv()
        for j in range(1, exp):
            second[k, j] = send(from_c[k], e, s2.at[k, j - 1], v2.at[k, j - 1], sides[j - 1])
        third.append(send(from_c[k], e, s3.at[k, 0], v3.at[k, 0], near))
    for k in range(ctx):
        for j in range(1, exp):
            second[k, j].wait_recv()
            third.append(send(from_c[k], from_e[j], s3.at[k, j], v3.at[k, j], near))
    for copy in third:
        copy.wait_recv()
    for copy in copies:
        copy.wait_send()


def gather_rows(own, ctx, exp, tp):
    whole = pl.BlockSpec(memory_space=pltpu.VMEM)
    counts = [(ctx - 1,), (ctx, exp - 1), (ctx, exp)]
    return pl.pallas_call(
        functools.partial(gather_kernel, ctx, exp, tp),
        out_shape=jax.ShapeDtypeStruct((ctx, exp, tp) + own.shape, own.dtype),
        in_specs=[whole],
        out_specs=whole,
        scratch_shapes=[pltpu.SemaphoreType.DMA(n) for n in counts for _ in range(2)],
        compiler_params=pltpu.CompilerParams(
            collective_id=2, has_side_effects=True, vmem_limit_bytes=VMEM_LIMIT
        ),
    )(own)


def down_kernel(active, weights, out):
    out[...] = jnp.dot(active[...], weights[...], preferred_element_type=jnp.float32).astype(jnp.bfloat16)


def down(active, weights):
    rows, hidden = active.shape
    width = weights.shape[1]
    tile = 512
    return pl.pallas_call(
        down_kernel,
        grid=(width // tile,),
        out_shape=jax.ShapeDtypeStruct((rows, width), jnp.bfloat16),
        in_specs=[
            pl.BlockSpec((rows, hidden), lambda i: (0, 0)),
            pl.BlockSpec((hidden, tile), lambda i: (0, i)),
        ],
        out_specs=pl.BlockSpec((rows, tile), lambda i: (0, i)),
        compiler_params=pltpu.CompilerParams(vmem_limit_bytes=VMEM_LIMIT),
    )(active, weights)


def shards(
    queries,
    rotated_key_heads,
    stored_value_heads,
    block_order,
    residual,
    out_weight,
    norm_gain,
    expert_ids,
    gate_logits,
    w_gate,
    w_up,
    w_down,
):
    ctx, exp, tp = (lax.axis_size(name) for name in ("ctx", "exp", "tp"))
    tok_rows, width = residual.shape
    local_experts = EXPERTS // exp
    all_axes = ("ctx", "exp", "tp")

    first = jax.nn.sigmoid(gate_logits[:, 0] - gate_logits[:, 1])
    second = jax.nn.sigmoid(gate_logits[:, 1] - gate_logits[:, 0])
    names = jnp.arange(EXPERTS, dtype=jnp.int32)[None, :]
    row_gates = first[:, None] * (expert_ids[:, :1] == names) + second[:, None] * (expert_ids[:, 1:] == names)

    qw, kw = queries.shape[1], rotated_key_heads.shape[1]
    own = jnp.concatenate([queries, rotated_key_heads, stored_value_heads], axis=1)
    qkv = lax.all_gather(own, "ctx", axis=0, tiled=True)
    attended = attend(qkv[:, :qw], qkv[:, qw : qw + kw], qkv[:, qw + kw :], block_order)
    part = jnp.dot(attended, out_weight, preferred_element_type=jnp.float32).astype(jnp.bfloat16)
    projected, gates = swap(
        part.reshape(ctx * exp * tp, tok_rows, -1),
        jnp.pad(row_gates, ((0, 0), (0, LANES - EXPERTS))),
        ctx,
        exp,
        tp,
    )
    gates = gates.reshape(-1, LANES)
    hidden_state = (residual.astype(jnp.float32) + projected).astype(jnp.bfloat16)
    state = hidden_state.astype(jnp.float32)
    normed = (
        state
        * lax.rsqrt(jnp.mean(state * state, axis=-1, keepdims=True) + 1e-05)
        * norm_gain.astype(jnp.float32)
    ).astype(jnp.bfloat16)

    rows = gather_rows(normed, ctx, exp, tp).reshape(-1, width)
    base = lax.axis_index("exp") * local_experts
    gate_val = jnp.einsum("rd,edf->erf", rows, w_gate, preferred_element_type=jnp.float32)
    up_val = jnp.einsum("rd,edf->erf", rows, w_up, preferred_element_type=jnp.float32)
    local_gates = lax.dynamic_slice_in_dim(gates, base, local_experts, axis=1)
    active = (jax.nn.silu(gate_val) * up_val * local_gates.T[:, :, None]).astype(jnp.bfloat16)
    active = jnp.transpose(active, (1, 0, 2)).reshape(rows.shape[0], -1)
    sums = down(active, w_down.reshape(-1, width))
    mixture = reduce_rows(sums.reshape(ctx, exp, tp, tok_rows, width))
    return (state + mixture).astype(jnp.bfloat16)


def solution(mesh):
    placed = (
        P(("grp", "ctx"), ("exp", "tp")),
        P(("grp", "ctx"), ("exp", "tp")),
        P(("grp", "ctx"), ("exp", "tp")),
        P("grp"),
        P(("grp", "ctx", "exp", "tp"), None),
        P(("exp", "tp"), "ctx"),
        P(),
        P(("grp", "ctx", "exp", "tp"), None),
        P(("grp", "ctx", "exp", "tp"), None),
        P("exp", None, ("ctx", "tp")),
        P("exp", None, ("ctx", "tp")),
        P("exp", ("ctx", "tp"), None),
    )
    return jax.shard_map(
        shards,
        mesh=mesh,
        in_specs=placed,
        out_specs=P(("grp", "ctx", "exp", "tp"), None),
        check_vma=False,
    )
```
